32 devices in a mesh: chan: 4 (over y, x), tm: 8 (over z, core).
Axes of the slice: x: 2, y: 2, z: 4, core: 2. Of those that a mesh axis runs over, the one named last changes fastest.
Arguments:
- traces: bfloat16 [64, 512, 2048], P('tm', 'chan'), may hold values from -6 to 6
- live: int32 [512], P('chan'), may hold values 0 or 1
Outputs:
- correlations: bfloat16 [512, 128, 2048], P(('chan', 'tm'))
The draws below stay inside these ranges and needn't reach their ends.
Inputs may be any that keep to these rules, and one draw needn't show every extreme that they name: `live`: 1 marks a usable channel, 0 a dead one.
All inputs are finite; a program needn't handle non-finite values. No bound on the sum of `live` on one device may be relied on, other than what follows from the above.
Results may differ from the reference program's by a relative error of at most 0.0076.
Values may be sent and summed in bfloat16 or wider, within the bound.
A program may use at most 128 MiB of HBM per device.

```python
import math
import jax
import jax.numpy as jnp
from jax import lax

BLOCK = 128
SAMPLES = 2048
SMOOTH = 4
FREQS = 1024
SEGMENTS = 64
CHANNELS = 512
N_CHAN = 4


def set_ends(values, own_key, low, largest):
    longest = values.shape.index(max(values.shape))
    spots = []
    for shift in (0, 1):
        where = [jax.random.randint(jax.random.fold_in(own_key, axis), (), 0, length) for axis, length in enumerate(values.shape)]
        where[longest] = (where[longest] + shift) % values.shape[longest]
        spots.append(tuple(where))
    return values.at[spots[0]].set(low).at[spots[1]].set(largest)


def levels(rng, shape, shards, least, high):
    def one(position, shards_of):
        steps = jax.random.uniform(jax.random.fold_in(jax.random.fold_in(rng, 6), position), (shards_of,), jnp.float32, least / len(shards), high / len(shards))
        return jnp.repeat(jnp.exp(steps), shape[position] // shards_of).reshape((-1,) + (1,) * (len(shape) - position - 1))

    loudness = one(*shards[0])
    for cut in shards[1:]:
        loudness = loudness * one(*cut)
    return loudness


def scatter_about(key, dims, scale, limit, cuts=(), kind=jnp.bfloat16):
    loudness = levels(key, dims, cuts, -0.22, 0.18) if cuts else 1.0
    array = jax.random.normal(key, dims, jnp.float32) * scale * loudness
    return jnp.minimum(jnp.maximum(array, -limit), limit).astype(kind)


def setup_inputs(seed: int = 0) -> dict:
    splits = jax.random.split(jax.random.key(seed), 3)
    traces = scatter_about(splits[0], (SEGMENTS, CHANNELS, SAMPLES), 1.0, 6.0, ((0, 8), (1, 4)))
    live = set_ends((jax.random.randint(splits[1], (CHANNELS,), 0, 8) < 7).astype(jnp.int32), jax.random.fold_in(splits[1], 1), 0, 1)
    return {"traces": traces, "live": live}


def column_bins(count, group_width):
    index = jnp.arange(count, dtype=jnp.int32)
    group = index // (2 * group_width)
    within = index % group_width
    is_imag = index // group_width % 2
    return (group * group_width + within, is_imag)

def forward_table(samples, bins, group_width):
    freq, is_imag = column_bins(2 * bins, group_width)
    moments = jnp.arange(samples, dtype=jnp.int32)[:, None]
    phase = (moments * freq[None, :] % samples).astype(jnp.float32) * (2.0 * math.pi / samples)
    return jnp.where(is_imag[None, :] == 1, -jnp.sin(phase), jnp.cos(phase)).astype(jnp.bfloat16)

def inverse_table(samples, bins, group_width, segments):
    freq, is_imag = column_bins(2 * bins, group_width)
    lag = jnp.arange(samples, dtype=jnp.int32) - samples // 2
    phase = jnp.mod(freq[:, None] * lag[None, :], samples).astype(jnp.float32) * (2.0 * math.pi / samples)
    weight = jnp.where(freq == 0, 1.0, 2.0).astype(jnp.float32) / math.sqrt(samples * segments)
    wave = jnp.where(is_imag[:, None] == 1, -jnp.sin(phase), jnp.cos(phase))
    return (weight[:, None] * wave).astype(jnp.bfloat16)

def whiten(spectra, groups):
    lead = spectra.shape[:-1]
    bins = spectra.shape[-1] // 2
    width = bins // groups
    split = spectra.reshape(lead + (groups, 2, width))
    real_part = split[..., 0, :].reshape(lead + (bins,))
    imag_part = split[..., 1, :].reshape(lead + (bins,))
    amplitude = jnp.sqrt(real_part * real_part + imag_part * imag_part)
    padded = jnp.pad(amplitude, [(0, 0)] * len(lead) + [(SMOOTH, SMOOTH)])
    smooth = sum((padded[..., i:i + bins] for i in range(2 * SMOOTH + 1))) / (2 * SMOOTH + 1)
    water = 0.8 * lax.optimization_barrier(jnp.mean(amplitude, axis=-1, keepdims=True)) + 1e-06
    level = jnp.maximum(smooth, water).reshape(lead + (groups, 1, width))
    return (split / level).reshape(lead + (2 * bins,)).astype(jnp.bfloat16)

def band(matrix):
    rows, width, extra = matrix.shape
    flat = matrix.reshape(rows * width, extra)
    flat = jnp.pad(flat, ((0, rows), (0, 0)))
    return flat.reshape(rows, width + 1, extra)[:, 1:rows + 1, :]

def cross(own_white, extended, own_flags, ext_flags, half):
    own_real = own_white[..., :half].astype(jnp.float32)
    own_imag = own_white[..., half:].astype(jnp.float32)
    ext_real = extended[..., :half].astype(jnp.float32)
    ext_imag = extended[..., half:].astype(jnp.float32)
    real_sum = jnp.einsum('sah,sbh->abh', own_real, ext_real) + jnp.einsum('sah,sbh->abh', own_imag, ext_imag)
    imag_sum = jnp.einsum('sah,sbh->abh', own_imag, ext_real) - jnp.einsum('sah,sbh->abh', own_real, ext_imag)
    pair_flags = band((own_flags[:, None] * ext_flags[None, :])[:, :, None])
    both = jnp.concatenate([band(real_sum), band(imag_sum)], axis=-1)
    return (both * pair_flags).astype(jnp.bfloat16)

def reference(traces, live):
    table = forward_table(SAMPLES, FREQS, FREQS)
    inverse = inverse_table(SAMPLES, FREQS, FREQS, SEGMENTS)
    blocks = traces.reshape(SEGMENTS, N_CHAN, BLOCK, SAMPLES).transpose(1, 0, 2, 3)

    def spectra_of(block_traces):
        spectra = jnp.dot(block_traces.reshape(SEGMENTS * BLOCK, SAMPLES), table, preferred_element_type=jnp.float32)
        return whiten(spectra.reshape(SEGMENTS, BLOCK, 2 * FREQS), 1)
    white = lax.map(spectra_of, blocks)
    following = jnp.concatenate([white[1:], jnp.zeros_like(white[:1])], axis=0)
    flags = live.reshape(N_CHAN, BLOCK).astype(jnp.float32)
    flags_next = jnp.concatenate([flags[1:], jnp.zeros_like(flags[:1])], axis=0)

    def correlate(items):
        own_white, next_white, own_flags, next_flags = items
        extended = jnp.concatenate([own_white, next_white], axis=1)
        ext_flags = jnp.concatenate([own_flags, next_flags], axis=0)
        stack = cross(own_white, extended, own_flags, ext_flags, FREQS)
        lagged = jnp.dot(stack.reshape(BLOCK * BLOCK, 2 * FREQS), inverse, preferred_element_type=jnp.float32)
        return lagged.astype(jnp.bfloat16).reshape(BLOCK, BLOCK, SAMPLES)
    result = lax.map(correlate, (white, following, flags, flags_next))
    return result.reshape(CHANNELS, BLOCK, SAMPLES)
```

```python
import functools
import math

import jax
import jax.numpy as jnp
import ml_dtypes
import numpy as np
from jax import lax
from jax.experimental import pallas as pl
from jax.experimental.pallas import tpu as pltpu
from jax.sharding import PartitionSpec as P

SMOOTH = 4
MIB = 1 << 20


def from_behind(block, axis, distance):
    devices = range(lax.axis_size(axis))
    route = [(i - distance, i) for i in devices if i - distance in devices]
    return lax.ppermute(block, axis, route)


def forward_rows(samples, bins):
    phase = np.outer(np.arange(bins), np.arange(samples)) % samples
    angle = phase * (2.0 * math.pi / samples)
    return np.concatenate([np.cos(angle), -np.sin(angle)], axis=0).astype(ml_dtypes.bfloat16)


def inverse_rows(samples, bins, groups, segments):
    lag = np.arange(samples) - samples // 2
    phase = np.mod(np.outer(np.arange(bins), lag), samples)
    angle = phase * (2.0 * math.pi / samples)
    weight = np.where(np.arange(bins) == 0, 1.0, 2.0)[:, None] / math.sqrt(samples * segments)
    width = bins // groups
    wave = np.stack([weight * np.cos(angle), -weight * np.sin(angle)])
    wave = wave.reshape(2, groups, width, samples).transpose(1, 0, 2, 3)
    return wave.reshape(2 * bins, samples).astype(ml_dtypes.bfloat16)


def whiten_kernel(pair, traces_ref, table_ref, white_ref, padded, held):
    _, block, samples = traces_ref.shape
    bins = samples // 2
    segs = held.shape[0] // bins // 2
    step = pl.program_id(0)
    rows = traces_ref[...].reshape(pair * block, samples)
    spectra = lax.dot_general(
        table_ref[...], rows, (((1,), (1,)), ((), ())), preferred_element_type=jnp.float32
    )
    real, imag = spectra[:bins], spectra[bins:]
    amplitude = jnp.sqrt(real * real + imag * imag)
    edge = jnp.zeros((8, pair * block), jnp.float32)
    padded[0:8, :] = edge
    padded[8 : 8 + bins, :] = amplitude
    padded[8 + bins :, :] = edge
    smooth = padded[8 - SMOOTH : 8 - SMOOTH + bins, :]
    for shift in range(1 - SMOOTH, SMOOTH + 1):
        smooth = smooth + padded[8 + shift : 8 + shift + bins, :]
    mean = jnp.sum(amplitude, axis=0, keepdims=True) * (1.0 / bins)
    level = jnp.maximum(smooth * (1.0 / (2 * SMOOTH + 1)), 0.8 * mean + 1e-06)
    scale = 1.0 / level
    for part, values in enumerate((real * scale, imag * scale)):
        for which in range(pair):
            row = part * segs + step * pair + which
            held[pl.ds(row, bins, stride=2 * segs), :] = values[
                :, which * block : (which + 1) * block
            ]

    @pl.when(step == pl.num_programs(0) - 1)
    def _():
        white_ref[...] = held[...].astype(jnp.bfloat16)


def whiten(traces, table):
    segs, block, samples = traces.shape
    bins = samples // 2
    pair = 2
    return pl.pallas_call(
        functools.partial(whiten_kernel, pair),
        grid=(segs // pair,),
        out_shape=jax.ShapeDtypeStruct((bins * 2 * segs, block), jnp.bfloat16),
        in_specs=[
            pl.BlockSpec((pair, block, samples), lambda i: (i, 0, 0)),
            pl.BlockSpec((2 * bins, samples), lambda i: (0, 0), pipeline_mode=pl.Buffered(1)),
        ],
        out_specs=pl.BlockSpec((bins * 2 * segs, block), lambda i: (0, 0)),
        scratch_shapes=[
            pltpu.VMEM((bins + 16, pair * block), jnp.float32),
            pltpu.VMEM((bins * 2 * segs, block), jnp.float32),
        ],
        compiler_params=pltpu.CompilerParams(vmem_limit_bytes=56 * MIB),
        cost_estimate=pl.CostEstimate(
            flops=2 * segs * block * samples * samples,
            bytes_accessed=2 * samples * samples + 4 * segs * block * samples,
            transcendentals=segs * block * bins,
        ),
        name="whiten",
    )(traces, table)


def skew(matrix):
    rows, _ = matrix.shape
    return pltpu.roll(matrix, rows, 1, stride=1, stride_axis=0)[:, :rows]


def cross_kernel(own_ref, next_ref, flag_ref, ext_ref, stack_ref, held):
    groups, width, depth, block = own_ref.shape
    half = depth // 2
    flags = skew(flag_ref[...] * ext_ref[...])
    down = lax.broadcasted_iota(jnp.int32, (block, block), 0)
    across = lax.broadcasted_iota(jnp.int32, (block, block), 1)
    reverse = jnp.where(down + across == block - 1, 1.0, 0.0).astype(jnp.bfloat16)

    def one(bin_index, carry):
        deep = groups * depth
        own = own_ref[:, bin_index].reshape(deep, block)
        back = jnp.dot(own, reverse, preferred_element_type=jnp.float32)
        split = back.reshape(groups, depth, block)
        turned = jnp.concatenate([split[:, half:], -split[:, :half]], axis=1)
        left = jnp.concatenate([back, turned.reshape(deep, block)], axis=1).astype(jnp.bfloat16)
        right = jnp.concatenate([own, next_ref[:, bin_index].reshape(deep, block)], axis=1)
        sums = lax.dot_general(
            left, right, (((0,), (0,)), ((), ())), preferred_element_type=jnp.float32
        )
        at = pl.ds(pl.multiple_of(bin_index * block, block), block)
        held[0, at, :] = skew(sums[:block]) * flags
        held[1, at, :] = skew(sums[block:]) * flags
        return carry

    lax.fori_loop(0, width, one, 0, unroll=4)
    rows = block // groups
    for part in range(2):
        for row in range(block):
            column = row % rows * block
            stack_ref[row // rows, part, :, column : column + block] = held[
                part, pl.ds(block - 1 - row, width, stride=block), :
            ].astype(jnp.bfloat16)


def cross(own, following, flags, ext_flags):
    groups, width, depth, block = own.shape
    step = 16
    spec = pl.BlockSpec((groups, step, depth, block), lambda i: (0, i, 0, 0))
    rows = block // groups * block
    return pl.pallas_call(
        cross_kernel,
        grid=(width // step,),
        out_shape=jax.ShapeDtypeStruct((groups, 2, width, rows), jnp.bfloat16),
        in_specs=[
            spec,
            spec,
            pl.BlockSpec((block, 1), lambda i: (0, 0)),
            pl.BlockSpec((1, 2 * block), lambda i: (0, 0)),
        ],
        out_specs=pl.BlockSpec((groups, 2, step, rows), lambda i: (0, 0, i, 0)),
        scratch_shapes=[pltpu.VMEM((2, step * block, block), jnp.float32)],
        compiler_params=pltpu.CompilerParams(vmem_limit_bytes=48 * MIB),
        cost_estimate=pl.CostEstimate(
            flops=8 * width * groups * depth * block * block,
            bytes_accessed=4 * own.size + 4 * width * block * block,
            transcendentals=0,
        ),
        name="cross",
    )(own, following, flags[::-1, None], ext_flags[None, :])


def body(traces, live):
    segs, block, samples = traces.shape
    bins = samples // 2
    groups = lax.axis_size("tm")
    width = bins // groups
    table = jnp.asarray(forward_rows(samples, bins))
    inverse = jnp.asarray(inverse_rows(samples, bins, groups, segs * groups))
    flags = live.astype(jnp.bfloat16)
    white = whiten(traces, table).reshape(groups, width, 2 * segs, block)
    own = lax.all_to_all(white, "tm", split_axis=0, concat_axis=0, tiled=True)
    following, next_flags = from_behind((own, flags), "chan", -1)
    ext_flags = jnp.concatenate([flags, next_flags], axis=0).astype(jnp.float32)
    stack = cross(own, following, flags.astype(jnp.float32), ext_flags)
    stack = lax.all_to_all(stack, "tm", split_axis=0, concat_axis=0, tiled=True)
    lagged = lax.dot_general(
        stack.reshape(2 * bins, block // groups * block),
        inverse,
        (((0,), (0,)), ((), ())),
        preferred_element_type=jnp.float32,
    )
    return lagged.astype(jnp.bfloat16).reshape(block // groups, block, samples)


def solution(mesh):
    in_specs = (P("tm", "chan", None), P("chan"))
    out_specs = P(("chan", "tm"), None, None)
    return jax.shard_map(body, mesh=mesh, in_specs=in_specs, out_specs=out_specs, check_vma=False)
```

```python
import functools
import math

import jax
import jax.numpy as jnp
import ml_dtypes
import numpy as np
from jax import lax
from jax.experimental import pallas as pl
from jax.experimental.pallas import tpu as pltpu
from jax.sharding import PartitionSpec as P

SMOOTH = 4
MIB = 1 << 20
CHUNKS = 4


def from_behind(block, axis, distance):
    devices = range(lax.axis_size(axis))
    route = [(i - distance, i) for i in devices if i - distance in devices]
    return lax.ppermute(block, axis, route)


def forward_rows(samples, bins):
    phase = np.outer(np.arange(bins), np.arange(samples)) % samples
    angle = phase * (2.0 * math.pi / samples)
    return np.concatenate([np.cos(angle), -np.sin(angle)], axis=0).astype(ml_dtypes.bfloat16)


def inverse_rows(samples, bins, groups, segments):
    lag = np.arange(samples) - samples // 2
    phase = np.mod(np.outer(np.arange(bins), lag), samples)
    angle = phase * (2.0 * math.pi / samples)
    weight = np.where(np.arange(bins) == 0, 1.0, 2.0)[:, None] / math.sqrt(samples * segments)
    width = bins // groups
    wave = np.stack([weight * np.cos(angle), -weight * np.sin(angle)])
    wave = wave.reshape(2, groups, width, samples).transpose(1, 0, 2, 3)
    return wave.reshape(2 * bins, samples).astype(ml_dtypes.bfloat16)


def whiten_kernel(pair, traces_ref, table_ref, white_ref, padded, held):
    _, block, samples = traces_ref.shape
    bins = samples // 2
    segs = held.shape[0] // bins // 2
    step = pl.program_id(0)
    rows = traces_ref[...].reshape(pair * block, samples)
    spectra = lax.dot_general(
        table_ref[...], rows, (((1,), (1,)), ((), ())), preferred_element_type=jnp.float32
    )
    real, imag = spectra[:bins], spectra[bins:]
    amplitude = jnp.sqrt(real * real + imag * imag)
    edge = jnp.zeros((8, pair * block), jnp.float32)
    padded[0:8, :] = edge
    padded[8 : 8 + bins, :] = amplitude
    padded[8 + bins :, :] = edge
    smooth = padded[8 - SMOOTH : 8 - SMOOTH + bins, :]
    for shift in range(1 - SMOOTH, SMOOTH + 1):
        smooth = smooth + padded[8 + shift : 8 + shift + bins, :]
    mean = jnp.sum(amplitude, axis=0, keepdims=True) * (1.0 / bins)
    level = jnp.maximum(smooth * (1.0 / (2 * SMOOTH + 1)), 0.8 * mean + 1e-06)
    scale = 1.0 / level
    for part, values in enumerate((real * scale, imag * scale)):
        for which in range(pair):
            row = part * segs + step * pair + which
            held[pl.ds(row, bins, stride=2 * segs), :] = values[
                :, which * block : (which + 1) * block
            ]

    @pl.when(step == pl.num_programs(0) - 1)
    def _():
        chunks, groups, rows, _ = white_ref.shape
        for group in range(groups):
            for chunk in range(chunks):
                first = (group * chunks + chunk) * rows
                white_ref[chunk, group] = held[first : first + rows, :].astype(jnp.bfloat16)


def whiten(traces, table, groups):
    segs, block, samples = traces.shape
    bins = samples // 2
    pair = 2
    rows = bins // groups // CHUNKS * 2 * segs
    return pl.pallas_call(
        functools.partial(whiten_kernel, pair),
        grid=(segs // pair,),
        out_shape=jax.ShapeDtypeStruct((CHUNKS, groups, rows, block), jnp.bfloat16),
        in_specs=[
            pl.BlockSpec((pair, block, samples), lambda i: (i, 0, 0)),
            pl.BlockSpec((2 * bins, samples), lambda i: (0, 0), pipeline_mode=pl.Buffered(1)),
        ],
        out_specs=pl.BlockSpec((CHUNKS, groups, rows, block), lambda i: (0, 0, 0, 0)),
        scratch_shapes=[
            pltpu.VMEM((bins + 16, pair * block), jnp.float32),
            pltpu.VMEM((bins * 2 * segs, block), jnp.float32),
        ],
        compiler_params=pltpu.CompilerParams(vmem_limit_bytes=56 * MIB),
        cost_estimate=pl.CostEstimate(
            flops=2 * segs * block * samples * samples,
            bytes_accessed=2 * samples * samples + 4 * segs * block * samples,
            transcendentals=segs * block * bins,
        ),
        name="whiten",
    )(traces, table)


def skew(matrix):
    rows, _ = matrix.shape
    return pltpu.roll(matrix, rows, 1, stride=1, stride_axis=0)[:, :rows]


def cross_chunk(own, following, flags, reverse, held, stack):
    groups, width, depth, block = own.shape
    half = depth // 2
    deep = groups * depth

    def one(bin_index, carry):
        mine = own[:, bin_index].reshape(deep, block)
        back = jnp.dot(mine, reverse, preferred_element_type=jnp.float32)
        split = back.reshape(groups, depth, block)
        turned = jnp.concatenate([split[:, half:], -split[:, :half]], axis=1)
        left = jnp.concatenate([back, turned.reshape(deep, block)], axis=1).astype(jnp.bfloat16)
        right = jnp.concatenate([mine, following[:, bin_index].reshape(deep, block)], axis=1)
        sums = lax.dot_general(
            left, right, (((0,), (0,)), ((), ())), preferred_element_type=jnp.float32
        )
        at = pl.ds(pl.multiple_of(bin_index * block, block), block)
        held[0, at, :] = skew(sums[:block]) * flags
        held[1, at, :] = skew(sums[block:]) * flags
        return carry

    lax.fori_loop(0, width, one, 0, unroll=4)
    rows = block // groups

    def spread(row, carry):
        column = pl.ds(pl.multiple_of(row * block, block), block)
        for group in range(groups):
            first = block - 1 - group * rows - row
            for part in range(2):
                stack[group, part, :, column] = held[
                    part, pl.ds(first, width, stride=block), :
                ].astype(jnp.bfloat16)
        return carry

    lax.fori_loop(0, rows, spread, 0)


def exchange_kernel(
    n_chan,
    white_ref,
    flag_ref,
    ext_ref,
    result_ref,
    own,
    following,
    stack,
    held,
    first_send,
    first_recv,
    shift_send,
    shift_recv,
    last_send,
    last_recv,
    local_sem,
):
    chunks, groups, _, _, block = own.shape
    me = lax.axis_index("tm")
    place = lax.axis_index("chan")
    before = lax.rem(place + n_chan - 1, n_chan)
    after = lax.rem(place + 1, n_chan)
    middle = groups // 2
    order = sorted(range(1, groups), key=lambda distance: abs(distance - middle))
    peers = [lax.rem(me + distance, groups) for distance in order]

    def first(chunk, peer, slot):
        return pltpu.make_async_remote_copy(
            src_ref=white_ref.at[chunk, peer],
            dst_ref=own.at[chunk, slot],
            send_sem=first_send.at[chunk, peer],
            recv_sem=first_recv.at[chunk, slot],
            device_id={"tm": peer},
            device_id_type=pl.DeviceIdType.MESH,
        )

    def shift(chunk):
        return pltpu.make_async_remote_copy(
            src_ref=own.at[chunk],
            dst_ref=following.at[chunk],
            send_sem=shift_send.at[chunk],
            recv_sem=shift_recv.at[chunk],
            device_id={"chan": before},
            device_id_type=pl.DeviceIdType.MESH,
        )

    def last(chunk, peer, slot):
        return pltpu.make_async_remote_copy(
            src_ref=stack.at[chunk, peer],
            dst_ref=result_ref.at[chunk, slot],
            send_sem=last_send.at[chunk, peer],
            recv_sem=last_recv.at[chunk, slot],
            device_id={"tm": peer},
            device_id_type=pl.DeviceIdType.MESH,
        )

    def keep_white(chunk):
        return pltpu.make_async_copy(
            white_ref.at[chunk, me], own.at[chunk, me], local_sem.at[0, chunk]
        )

    def keep_stack(chunk):
        return pltpu.make_async_copy(
            stack.at[chunk, me], result_ref.at[chunk, me], local_sem.at[1, chunk]
        )

    barrier = pltpu.get_barrier_semaphore()
    for peer in peers:
        pl.semaphore_signal(
            barrier, inc=1, device_id={"tm": peer}, device_id_type=pl.DeviceIdType.MESH
        )
    for neighbour in (before, after):
        pl.semaphore_signal(
            barrier, inc=1, device_id={"chan": neighbour}, device_id_type=pl.DeviceIdType.MESH
        )
    pl.semaphore_wait(barrier, groups + 1)

    def start_first(chunk):
        for peer in peers:
            first(chunk, peer, me).start()
        keep_white(chunk).start()

    def arrive(chunk):
        for peer in peers:
            first(chunk, peer, peer).wait_recv()
        keep_white(chunk).wait()
        shift(chunk).start()

    def work(chunk):
        shift(chunk).wait_recv()
        cross_chunk(own.at[chunk], following.at[chunk], flags, reverse, held, stack.at[chunk])
        for peer in peers:
            last(chunk, peer, me).start()
        keep_stack(chunk).start()

    start_first(0)
    start_first(1)
    flags = skew(flag_ref[...] * ext_ref[...])
    down = lax.broadcasted_iota(jnp.int32, (block, block), 0)
    across = lax.broadcasted_iota(jnp.int32, (block, block), 1)
    reverse = jnp.where(down + across == block - 1, 1.0, 0.0).astype(jnp.bfloat16)
    for chunk in range(chunks):
        arrive(chunk)
        if chunk + 2 < chunks:
            start_first(chunk + 2)
        if chunk >= 1:
            work(chunk - 1)
    work(chunks - 1)
    for chunk in range(chunks):
        for peer in peers:
            first(chunk, peer, peer).wait_send()
            last(chunk, peer, peer).wait_send()
            last(chunk, peer, peer).wait_recv()
        shift(chunk).wait_send()
        keep_stack(chunk).wait()


def exchange(white, flags, ext_flags):
    chunks, groups, width, depth, block = white.shape
    rows = block // groups * block
    stack = (chunks, groups, 2, width, rows)
    dma = pltpu.SemaphoreType.DMA
    return pl.pallas_call(
        functools.partial(exchange_kernel, lax.axis_size("chan")),
        out_shape=jax.ShapeDtypeStruct(stack, jnp.bfloat16),
        in_specs=[
            pl.BlockSpec(memory_space=pl.ANY),
            pl.BlockSpec(memory_space=pltpu.VMEM),
            pl.BlockSpec(memory_space=pltpu.VMEM),
        ],
        out_specs=pl.BlockSpec(memory_space=pl.ANY),
        scratch_shapes=[
            pltpu.VMEM(white.shape, jnp.bfloat16),
            pltpu.VMEM(white.shape, jnp.bfloat16),
            pltpu.VMEM(stack, jnp.bfloat16),
            pltpu.VMEM((2, width * block, block), jnp.float32),
            dma((chunks, groups)),
            dma((chunks, groups)),
            dma((chunks,)),
            dma((chunks,)),
            dma((chunks, groups)),
            dma((chunks, groups)),
            dma((2, chunks)),
        ],
        compiler_params=pltpu.CompilerParams(
            vmem_limit_bytes=52 * MIB, collective_id=0, has_side_effects=True
        ),
        cost_estimate=pl.CostEstimate(
            flops=8 * chunks * width * groups * depth * block * block,
            bytes_accessed=8 * white.size,
            transcendentals=0,
        ),
        name="exchange",
    )(white, flags[::-1, None], ext_flags[None, :])


def body(traces, live):
    segs, block, samples = traces.shape
    bins = samples // 2
    groups = lax.axis_size("tm")
    width = bins // groups
    table = jnp.asarray(forward_rows(samples, bins))
    inverse = inverse_rows(samples, bins, groups, segs * groups)
    inverse = inverse.reshape(groups, 2, CHUNKS, width // CHUNKS, samples)
    inverse = inverse.transpose(2, 0, 1, 3, 4).reshape(2 * bins, samples)
    flags = live.astype(jnp.bfloat16)
    next_flags = from_behind(flags, "chan", -1)
    ext_flags = jnp.concatenate([flags, next_flags], axis=0).astype(jnp.float32)
    own_flags = flags.astype(jnp.float32)
    part = width // CHUNKS
    white = whiten(traces, table, groups).reshape(CHUNKS, groups, part, 2 * segs, block)
    stack = exchange(white, own_flags, ext_flags)
    lagged = lax.dot_general(
        stack.reshape(2 * bins, block // groups * block),
        jnp.asarray(inverse),
        (((0,), (0,)), ((), ())),
        preferred_element_type=jnp.float32,
    )
    return lagged.astype(jnp.bfloat16).reshape(block // groups, block, samples)


def solution(mesh):
    in_specs = (P("tm", "chan", None), P("chan"))
    out_specs = P(("chan", "tm"), None, None)
    return jax.shard_map(body, mesh=mesh, in_specs=in_specs, out_specs=out_specs, check_vma=False)
```

```python
import functools
import math

import jax
import jax.numpy as jnp
import ml_dtypes
import numpy as np
from jax import lax
from jax.experimental import pallas as pl
from jax.experimental.pallas import tpu as pltpu
from jax.sharding import PartitionSpec as P

SMOOTH = 4
MIB = 1 << 20
CHUNKS = 8
SPANS = 2


def from_behind(block, axis, distance):
    devices = range(lax.axis_size(axis))
    route = [(i - distance, i) for i in devices if i - distance in devices]
    return lax.ppermute(block, axis, route)


def forward_rows(samples, bins):
    phase = np.outer(np.arange(bins), np.arange(samples)) % samples
    angle = phase * (2.0 * math.pi / samples)
    return np.concatenate([np.cos(angle), -np.sin(angle)], axis=0).astype(ml_dtypes.bfloat16)


def inverse_rows(samples, bins, groups, segments):
    lag = np.arange(samples) - samples // 2
    phase = np.mod(np.outer(np.arange(bins), lag), samples)
    angle = phase * (2.0 * math.pi / samples)
    weight = np.where(np.arange(bins) == 0, 1.0, 2.0)[:, None] / math.sqrt(samples * segments)
    width = bins // groups
    wave = np.stack([weight * np.cos(angle), -weight * np.sin(angle)])
    wave = wave.reshape(2, groups, width, samples).transpose(1, 0, 2, 3)
    return wave.reshape(2 * bins, samples).astype(ml_dtypes.bfloat16)


def whiten_kernel(pair, traces_ref, table_ref, white_ref, padded, held):
    _, block, samples = traces_ref.shape
    bins = samples // 2
    segs = held.shape[0] // bins // 2
    step = pl.program_id(0)
    rows = traces_ref[...].reshape(pair * block, samples)
    spectra = lax.dot_general(
        table_ref[...], rows, (((1,), (1,)), ((), ())), preferred_element_type=jnp.float32
    )
    real, imag = spectra[:bins], spectra[bins:]
    amplitude = jnp.sqrt(real * real + imag * imag)
    edge = jnp.zeros((8, pair * block), jnp.float32)
    padded[0:8, :] = edge
    padded[8 : 8 + bins, :] = amplitude
    padded[8 + bins :, :] = edge
    smooth = padded[8 - SMOOTH : 8 - SMOOTH + bins, :]
    for shift in range(1 - SMOOTH, SMOOTH + 1):
        smooth = smooth + padded[8 + shift : 8 + shift + bins, :]
    mean = jnp.sum(amplitude, axis=0, keepdims=True) * (1.0 / bins)
    level = jnp.maximum(smooth * (1.0 / (2 * SMOOTH + 1)), 0.8 * mean + 1e-06)
    scale = 1.0 / level
    for part, values in enumerate((real * scale, imag * scale)):
        for which in range(pair):
            row = part * segs + step * pair + which
            held[pl.ds(row, bins, stride=2 * segs), :] = values[
                :, which * block : (which + 1) * block
            ]

    @pl.when(step == pl.num_programs(0) - 1)
    def _():
        chunks, groups, rows, _ = white_ref.shape
        for group in range(groups):
            for chunk in range(chunks):
                first = (group * chunks + chunk) * rows
                white_ref[chunk, group] = held[first : first + rows, :].astype(jnp.bfloat16)


def whiten(traces, table, groups):
    segs, block, samples = traces.shape
    bins = samples // 2
    pair = 2
    rows = bins // groups // CHUNKS * 2 * segs
    return pl.pallas_call(
        functools.partial(whiten_kernel, pair),
        grid=(segs // pair,),
        out_shape=jax.ShapeDtypeStruct((CHUNKS, groups, rows, block), jnp.bfloat16),
        in_specs=[
            pl.BlockSpec((pair, block, samples), lambda i: (i, 0, 0)),
            pl.BlockSpec((2 * bins, samples), lambda i: (0, 0), pipeline_mode=pl.Buffered(1)),
        ],
        out_specs=pl.BlockSpec((CHUNKS, groups, rows, block), lambda i: (0, 0, 0, 0)),
        scratch_shapes=[
            pltpu.VMEM((bins + 16, pair * block), jnp.float32),
            pltpu.VMEM((bins * 2 * segs, block), jnp.float32),
        ],
        compiler_params=pltpu.CompilerParams(vmem_limit_bytes=56 * MIB),
        cost_estimate=pl.CostEstimate(
            flops=2 * segs * block * samples * samples,
            bytes_accessed=2 * samples * samples + 4 * segs * block * samples,
            transcendentals=segs * block * bins,
        ),
        name="whiten",
    )(traces, table)


def skew(matrix, shift, columns):
    return pltpu.roll(matrix, shift, 1, stride=1, stride_axis=0)[:, :columns]


def cross_chunk(own, following, flags, shift, reverse, held, stack):
    groups, width, depth, block = own.shape
    members = stack.shape[0]
    rows = held.shape[1] // width
    share = rows // members
    half = depth // 2
    deep = groups * depth
    lane = lax.broadcasted_iota(jnp.int32, (1, 1, 2 * rows), 2)

    def one(bin_index, carry):
        mine = own[:, bin_index].reshape(deep, block)
        back = jnp.dot(mine, reverse, preferred_element_type=jnp.float32)
        back = back.reshape(groups, depth, 2 * rows)
        turned = jnp.concatenate([back[:, half:], -back[:, :half]], axis=1)
        left = jnp.where(lane < rows, back, turned).reshape(deep, 2 * rows).astype(jnp.bfloat16)
        right = jnp.concatenate([mine, following[:, bin_index].reshape(deep, block)], axis=1)
        sums = lax.dot_general(
            left, right, (((0,), (0,)), ((), ())), preferred_element_type=jnp.float32
        )
        at = pl.ds(pl.multiple_of(bin_index * rows, rows), rows)
        held[0, at, :] = skew(sums[:rows], shift, block) * flags
        held[1, at, :] = skew(sums[rows:], shift, block) * flags
        return carry

    lax.fori_loop(0, width, one, 0, unroll=4)

    def spread(row, carry):
        column = pl.ds(pl.multiple_of(row * block, block), block)
        for member in range(members):
            first = rows - 1 - member * share - row
            for part in range(2):
                stack[member, part, :, column] = held[
                    part, pl.ds(first, width, stride=rows), :
                ].astype(jnp.bfloat16)
        return carry

    lax.fori_loop(0, share, spread, 0)


def exchange_kernel(
    n_chan,
    white_ref,
    flag_ref,
    ext_ref,
    result_ref,
    own,
    following,
    stack,
    held,
    first_send,
    first_recv,
    shift_send,
    shift_recv,
    last_send,
    last_recv,
    local_sem,
):
    chunks, groups, width, _, block = own.shape
    members = groups // SPANS
    rows = block // SPANS
    me = lax.axis_index("tm")
    place = lax.axis_index("chan")
    before = lax.rem(place + n_chan - 1, n_chan)
    after = lax.rem(place + 1, n_chan)
    middle = groups // 2
    order = sorted(range(1, groups), key=lambda distance: abs(distance - middle))
    peers = [lax.rem(me + distance, groups) for distance in order]
    span = me // members
    mine = lax.rem(me, members)
    mates = [lax.rem(mine + distance, members) for distance in range(1, members)]

    def first(chunk, peer, slot):
        return pltpu.make_async_remote_copy(
            src_ref=white_ref.at[chunk, lax.rem(peer, members)],
            dst_ref=own.at[chunk, slot],
            send_sem=first_send.at[chunk, peer],
            recv_sem=first_recv.at[chunk, slot],
            device_id={"tm": peer},
            device_id_type=pl.DeviceIdType.MESH,
        )

    def shift(chunk):
        return pltpu.make_async_remote_copy(
            src_ref=own.at[chunk],
            dst_ref=following.at[chunk],
            send_sem=shift_send.at[chunk],
            recv_sem=shift_recv.at[chunk],
            device_id={"chan": before},
            device_id_type=pl.DeviceIdType.MESH,
        )

    def last(chunk, mate, slot):
        return pltpu.make_async_remote_copy(
            src_ref=stack.at[chunk, mate],
            dst_ref=result_ref.at[chunk, slot],
            send_sem=last_send.at[chunk, mate],
            recv_sem=last_recv.at[chunk, slot],
            device_id={"tm": span * members + mate},
            device_id_type=pl.DeviceIdType.MESH,
        )

    def keep_white(chunk):
        return pltpu.make_async_copy(
            white_ref.at[chunk, mine], own.at[chunk, me], local_sem.at[0, chunk]
        )

    def keep_stack(chunk):
        return pltpu.make_async_copy(
            stack.at[chunk, mine], result_ref.at[chunk, mine], local_sem.at[1, chunk]
        )

    barrier = pltpu.get_barrier_semaphore()
    for peer in peers:
        pl.semaphore_signal(
            barrier, inc=1, device_id={"tm": peer}, device_id_type=pl.DeviceIdType.MESH
        )
    for neighbour in (before, after):
        pl.semaphore_signal(
            barrier, inc=1, device_id={"chan": neighbour}, device_id_type=pl.DeviceIdType.MESH
        )
    pl.semaphore_wait(barrier, groups + 1)

    def start_first(chunk):
        for peer in peers:
            first(chunk, peer, me).start()
        keep_white(chunk).start()

    def arrive(chunk):
        for peer in peers:
            first(chunk, peer, peer).wait_recv()
        keep_white(chunk).wait()
        shift(chunk).start()

    def work(chunk):
        shift(chunk).wait_recv()
        for which in range(SPANS):

            @pl.when(span == which)
            def _():
                turn = 2 * block - (which + 1) * rows
                flags = skew(flag_ref[...] * ext_ref[...], turn, block)
                cross_chunk(
                    own.at[chunk], following.at[chunk], flags, turn, reverse, held, stack.at[chunk]
                )

        for mate in mates:
            last(chunk, mate, mine).start()
        keep_stack(chunk).start()

    start_first(0)
    start_first(1)
    down = lax.broadcasted_iota(jnp.int32, (block, 2 * rows), 0)
    across = lax.broadcasted_iota(jnp.int32, (block, 2 * rows), 1) % rows
    reverse = jnp.where(down + across == (span + 1) * rows - 1, 1.0, 0.0).astype(jnp.bfloat16)
    for chunk in range(chunks):
        arrive(chunk)
        if chunk + 2 < chunks:
            start_first(chunk + 2)
        if chunk >= 1:
            work(chunk - 1)
    work(chunks - 1)
    for chunk in range(chunks):
        for peer in peers:
            first(chunk, peer, peer).wait_send()
        for mate in mates:
            last(chunk, mate, mate).wait_send()
            last(chunk, mate, mate).wait_recv()
        shift(chunk).wait_send()
        keep_stack(chunk).wait()


def exchange(white, flags, ext_flags):
    chunks, members, width, depth, block = white.shape
    groups = members * SPANS
    gathered = (chunks, groups, width, depth, block)
    stack = (chunks, members, 2, width, block // groups * block)
    dma = pltpu.SemaphoreType.DMA
    return pl.pallas_call(
        functools.partial(exchange_kernel, lax.axis_size("chan")),
        out_shape=jax.ShapeDtypeStruct(stack, jnp.bfloat16),
        in_specs=[
            pl.BlockSpec(memory_space=pl.ANY),
            pl.BlockSpec(memory_space=pltpu.VMEM),
            pl.BlockSpec(memory_space=pltpu.VMEM),
        ],
        out_specs=pl.BlockSpec(memory_space=pl.ANY),
        scratch_shapes=[
            pltpu.VMEM(gathered, jnp.bfloat16),
            pltpu.VMEM(gathered, jnp.bfloat16),
            pltpu.VMEM(stack, jnp.bfloat16),
            pltpu.VMEM((2, width * (block // SPANS), block), jnp.float32),
            dma((chunks, groups)),
            dma((chunks, groups)),
            dma((chunks,)),
            dma((chunks,)),
            dma((chunks, members)),
            dma((chunks, members)),
            dma((2, chunks)),
        ],
        compiler_params=pltpu.CompilerParams(
            vmem_limit_bytes=52 * MIB, collective_id=0, has_side_effects=True
        ),
        cost_estimate=pl.CostEstimate(
            flops=8 * chunks * width * groups * depth * block * block,
            bytes_accessed=12 * white.size,
            transcendentals=0,
        ),
        name="exchange",
    )(white, flags[:, None], ext_flags[None, :])


def body(traces, live):
    segs, block, samples = traces.shape
    bins = samples // 2
    groups = lax.axis_size("tm")
    members = groups // SPANS
    part = bins // members // CHUNKS
    table = jnp.asarray(forward_rows(samples, bins))
    inverse = inverse_rows(samples, bins, members, segs * groups)
    inverse = inverse.reshape(members, 2, CHUNKS, part, samples)
    inverse = inverse.transpose(2, 0, 1, 3, 4).reshape(2 * bins, samples)
    flags = live.astype(jnp.bfloat16)
    next_flags = from_behind(flags, "chan", -1)
    ext_flags = jnp.concatenate([flags, next_flags], axis=0).astype(jnp.float32)
    rows = block // SPANS
    span = lax.axis_index("tm") // members
    span_flags = lax.dynamic_slice(flags.astype(jnp.float32), (span * rows,), (rows,))[::-1]
    white = whiten(traces, table, members).reshape(CHUNKS, members, part, 2 * segs, block)
    stack = exchange(white, span_flags, ext_flags)
    lagged = lax.dot_general(
        stack.reshape(2 * bins, block // groups * block),
        jnp.asarray(inverse),
        (((0,), (0,)), ((), ())),
        preferred_element_type=jnp.float32,
    )
    return lagged.astype(jnp.bfloat16).reshape(block // groups, block, samples)


def solution(mesh):
    in_specs = (P("tm", "chan", None), P("chan"))
    out_specs = P(("chan", "tm"), None, None)
    return jax.shard_map(body, mesh=mesh, in_specs=in_specs, out_specs=out_specs, check_vma=False)
```

```python
import functools
import math

import jax
import jax.numpy as jnp
import ml_dtypes
import numpy as np
from jax import lax
from jax.experimental import pallas as pl
from jax.experimental.pallas import tpu as pltpu
from jax.sharding import PartitionSpec as P

SMOOTH = 4
MIB = 1 << 20
PART = 16
SPANS = 2
AHEAD = 3


def from_behind(block, axis, distance):
    devices = range(lax.axis_size(axis))
    route = [(i - distance, i) for i in devices if i - distance in devices]
    return lax.ppermute(block, axis, route)


def forward_rows(samples, bins):
    phase = np.outer(np.arange(bins), np.arange(samples)) % samples
    angle = phase * (2.0 * math.pi / samples)
    return np.concatenate([np.cos(angle), -np.sin(angle)], axis=0).astype(ml_dtypes.bfloat16)


def inverse_rows(samples, bins, groups, segments):
    lag = np.arange(samples) - samples // 2
    phase = np.mod(np.outer(np.arange(bins), lag), samples)
    angle = phase * (2.0 * math.pi / samples)
    weight = np.where(np.arange(bins) == 0, 1.0, 2.0)[:, None] / math.sqrt(samples * segments)
    width = bins // groups
    wave = np.stack([weight * np.cos(angle), -weight * np.sin(angle)])
    wave = wave.reshape(2, groups, width, samples).transpose(1, 0, 2, 3)
    return wave.reshape(2 * bins, samples).astype(ml_dtypes.bfloat16)


def whiten_kernel(pair, traces_ref, table_ref, white_ref, spectra, padded, held):
    count, block, samples = traces_ref.shape
    bins = samples // 2
    segs = held.shape[0] // bins // 2
    lanes = pair * block
    origin = pl.program_id(0) * count
    edge = jnp.zeros((8, lanes), jnp.float32)
    for slot in range(2):
        padded[slot, 0:8, :] = edge
        padded[slot, 8 + bins :, :] = edge

    def transform(step):
        rows = traces_ref[step * pair : (step + 1) * pair].reshape(lanes, samples)
        spectra[step % 2] = lax.dot_general(
            table_ref[...], rows, (((1,), (1,)), ((), ())), preferred_element_type=jnp.float32
        )

    def finish(step):
        slot = step % 2
        real, imag = spectra[slot, :bins], spectra[slot, bins:]
        amplitude = jnp.sqrt(real * real + imag * imag)
        padded[slot, 8 : 8 + bins, :] = amplitude
        smooth = padded[slot, 8 - SMOOTH : 8 - SMOOTH + bins, :]
        for shift in range(1 - SMOOTH, SMOOTH + 1):
            smooth = smooth + padded[slot, 8 + shift : 8 + shift + bins, :]
        mean = jnp.sum(amplitude, axis=0, keepdims=True) * (1.0 / bins)
        level = jnp.maximum(smooth * (1.0 / (2 * SMOOTH + 1)), 0.8 * mean + 1e-06)
        scale = 1.0 / level
        for part, values in enumerate((real * scale, imag * scale)):
            for which in range(pair):
                row = part * segs + origin + step * pair + which
                held[pl.ds(row, bins, stride=2 * segs), :] = values[
                    :, which * block : (which + 1) * block
                ]

    steps = count // pair
    transform(0)
    for step in range(steps):
        if step + 1 < steps:
            transform(step + 1)
        finish(step)

    @pl.when(pl.program_id(0) == pl.num_programs(0) - 1)
    def _():
        chunks, groups, rows, _ = white_ref.shape
        for group in range(groups):
            for chunk in range(chunks):
                first = (group * chunks + chunk) * rows
                white_ref[chunk, group] = held[first : first + rows, :].astype(jnp.bfloat16)


def whiten(traces, table, groups):
    segs, block, samples = traces.shape
    bins = samples // 2
    pair = 2
    rows = PART * 2 * segs
    chunks = bins // groups // PART
    return pl.pallas_call(
        functools.partial(whiten_kernel, pair),
        grid=(segs // (2 * pair),),
        out_shape=jax.ShapeDtypeStruct((chunks, groups, rows, block), jnp.bfloat16),
        in_specs=[
            pl.BlockSpec((2 * pair, block, samples), lambda i: (i, 0, 0)),
            pl.BlockSpec((2 * bins, samples), lambda i: (0, 0), pipeline_mode=pl.Buffered(1)),
        ],
        out_specs=pl.BlockSpec((chunks, groups, rows, block), lambda i: (0, 0, 0, 0)),
        scratch_shapes=[
            pltpu.VMEM((2, 2 * bins, pair * block), jnp.float32),
            pltpu.VMEM((2, bins + 16, pair * block), jnp.float32),
            pltpu.VMEM((bins * 2 * segs, block), jnp.float32),
        ],
        compiler_params=pltpu.CompilerParams(vmem_limit_bytes=56 * MIB),
        cost_estimate=pl.CostEstimate(
            flops=2 * segs * block * samples * samples,
            bytes_accessed=2 * samples * samples + 4 * segs * block * samples,
            transcendentals=segs * block * bins,
        ),
        name="whiten",
    )(traces, table)


def skew(matrix, shift, columns):
    return pltpu.roll(matrix, shift, 1, stride=1, stride_axis=0)[:, :columns]


def cross_chunk(own, following, flags, shift, reverse, held, stack):
    groups, width, depth, block = own.shape
    members = stack.shape[0]
    rows = held.shape[1] // width
    share = rows // members
    half = depth // 2
    deep = groups * depth
    lane = lax.broadcasted_iota(jnp.int32, (1, 1, 2 * rows), 2)

    def one(bin_index, carry):
        mine = own[:, bin_index].reshape(deep, block)
        back = jnp.dot(mine, reverse, preferred_element_type=jnp.float32)
        back = back.reshape(groups, depth, 2 * rows)
        turned = jnp.concatenate([back[:, half:], -back[:, :half]], axis=1)
        left = jnp.where(lane < rows, back, turned).reshape(deep, 2 * rows).astype(jnp.bfloat16)
        right = jnp.concatenate([mine, following[:, bin_index].reshape(deep, block)], axis=1)
        sums = lax.dot_general(
            left, right, (((0,), (0,)), ((), ())), preferred_element_type=jnp.float32
        )
        at = pl.ds(pl.multiple_of(bin_index * rows, rows), rows)
        held[0, at, :] = skew(sums[:rows], shift, block) * flags
        held[1, at, :] = skew(sums[rows:], shift, block) * flags
        return carry

    lax.fori_loop(0, width, one, 0, unroll=4)

    def spread(row, carry):
        column = pl.ds(pl.multiple_of(row * block, block), block)
        for member in range(members):
            first = rows - 1 - member * share - row
            for part in range(2):
                stack[member, part, :, column] = held[
                    part, pl.ds(first, width, stride=rows), :
                ].astype(jnp.bfloat16)
        return carry

    lax.fori_loop(0, share, spread, 0)


def exchange_kernel(
    n_chan,
    white_ref,
    flag_ref,
    ext_ref,
    result_ref,
    own,
    following,
    stack,
    held,
    first_send,
    first_recv,
    shift_send,
    shift_recv,
    last_send,
    last_recv,
    local_sem,
):
    chunks, groups, width, _, block = own.shape
    members = groups // SPANS
    rows = block // SPANS
    me = lax.axis_index("tm")
    place = lax.axis_index("chan")
    before = lax.rem(place + n_chan - 1, n_chan)
    after = lax.rem(place + 1, n_chan)
    middle = groups // 2
    order = sorted(range(1, groups), key=lambda distance: abs(distance - middle))
    peers = [lax.rem(me + distance, groups) for distance in order]
    span = me // members
    mine = lax.rem(me, members)
    mates = [lax.rem(mine + distance, members) for distance in range(1, members)]

    def first(chunk, peer, slot):
        return pltpu.make_async_remote_copy(
            src_ref=white_ref.at[chunk, lax.rem(peer, members)],
            dst_ref=own.at[chunk, slot],
            send_sem=first_send.at[chunk, peer],
            recv_sem=first_recv.at[chunk, slot],
            device_id={"tm": peer},
            device_id_type=pl.DeviceIdType.MESH,
        )

    def shift(chunk, slot):
        return pltpu.make_async_remote_copy(
            src_ref=own.at[chunk, slot],
            dst_ref=following.at[chunk, slot],
            send_sem=shift_send.at[chunk, slot],
            recv_sem=shift_recv.at[chunk, slot],
            device_id={"chan": before},
            device_id_type=pl.DeviceIdType.MESH,
        )

    def last(chunk, mate, slot):
        return pltpu.make_async_remote_copy(
            src_ref=stack.at[chunk, mate],
            dst_ref=result_ref.at[chunk, slot],
            send_sem=last_send.at[chunk, mate],
            recv_sem=last_recv.at[chunk, slot],
            device_id={"tm": span * members + mate},
            device_id_type=pl.DeviceIdType.MESH,
        )

    def keep_white(chunk):
        return pltpu.make_async_copy(
            white_ref.at[chunk, mine], own.at[chunk, me], local_sem.at[0, chunk]
        )

    def keep_stack(chunk):
        return pltpu.make_async_copy(
            stack.at[chunk, mine], result_ref.at[chunk, mine], local_sem.at[1, chunk]
        )

    barrier = pltpu.get_barrier_semaphore()
    for peer in peers:
        pl.semaphore_signal(
            barrier, inc=1, device_id={"tm": peer}, device_id_type=pl.DeviceIdType.MESH
        )
    for neighbour in (before, after):
        pl.semaphore_signal(
            barrier, inc=1, device_id={"chan": neighbour}, device_id_type=pl.DeviceIdType.MESH
        )
    pl.semaphore_wait(barrier, groups + 1)

    def start_first(chunk):
        for peer in peers:
            first(chunk, peer, me).start()
        keep_white(chunk).start()

    def arrive(chunk):
        keep_white(chunk).wait()
        shift(chunk, me).start()
        for peer in peers[::-1]:
            first(chunk, peer, peer).wait_recv()
            shift(chunk, peer).start()

    def work(chunk):
        for slot in range(groups):
            shift(chunk, slot).wait_recv()
        for which in range(SPANS):

            @pl.when(span == which)
            def _():
                turn = 2 * block - (which + 1) * rows
                flags = skew(flag_ref[...] * ext_ref[...], turn, block)
                cross_chunk(
                    own.at[chunk], following.at[chunk], flags, turn, reverse, held, stack.at[chunk]
                )

        for mate in mates:
            last(chunk, mate, mine).start()
        keep_stack(chunk).start()

    for chunk in range(AHEAD):
        start_first(chunk)
    down = lax.broadcasted_iota(jnp.int32, (block, 2 * rows), 0)
    across = lax.broadcasted_iota(jnp.int32, (block, 2 * rows), 1) % rows
    reverse = jnp.where(down + across == (span + 1) * rows - 1, 1.0, 0.0).astype(jnp.bfloat16)
    arrive(0)

    def steady(chunk, carry):
        arrive(chunk)
        start_first(chunk + AHEAD)
        work(chunk - 1)
        return carry

    def drain(chunk, carry):
        arrive(chunk)
        work(chunk - 1)
        return carry

    def finish(chunk, carry):
        for peer in peers:
            first(chunk, peer, peer).wait_send()
        for mate in mates:
            last(chunk, mate, mate).wait_send()
            last(chunk, mate, mate).wait_recv()
        for slot in range(groups):
            shift(chunk, slot).wait_send()
        keep_stack(chunk).wait()
        return carry

    steady_end = chunks - AHEAD
    start_first(AHEAD)
    lax.fori_loop(1, steady_end, steady, 0)
    lax.fori_loop(steady_end, chunks, drain, 0)
    work(chunks - 1)
    lax.fori_loop(0, chunks, finish, 0)


def exchange(white, flags, ext_flags):
    chunks, members, width, depth, block = white.shape
    groups = members * SPANS
    gathered = (chunks, groups, width, depth, block)
    stack = (chunks, members, 2, width, block // groups * block)
    dma = pltpu.SemaphoreType.DMA
    return pl.pallas_call(
        functools.partial(exchange_kernel, lax.axis_size("chan")),
        out_shape=jax.ShapeDtypeStruct(stack, jnp.bfloat16),
        in_specs=[
            pl.BlockSpec(memory_space=pl.ANY),
            pl.BlockSpec(memory_space=pltpu.VMEM),
            pl.BlockSpec(memory_space=pltpu.VMEM),
        ],
        out_specs=pl.BlockSpec(memory_space=pl.ANY),
        scratch_shapes=[
            pltpu.VMEM(gathered, jnp.bfloat16),
            pltpu.VMEM(gathered, jnp.bfloat16),
            pltpu.VMEM(stack, jnp.bfloat16),
            pltpu.VMEM((2, width * (block // SPANS), block), jnp.float32),
            dma((chunks, groups)),
            dma((chunks, groups)),
            dma((chunks, groups)),
            dma((chunks, groups)),
            dma((chunks, members)),
            dma((chunks, members)),
            dma((2, chunks)),
        ],
        compiler_params=pltpu.CompilerParams(
            vmem_limit_bytes=52 * MIB, collective_id=0, has_side_effects=True
        ),
        cost_estimate=pl.CostEstimate(
            flops=8 * chunks * width * groups * depth * block * block,
            bytes_accessed=12 * white.size,
            transcendentals=0,
        ),
        name="exchange",
    )(white, flags[:, None], ext_flags[None, :])


def body(traces, live):
    segs, block, samples = traces.shape
    bins = samples // 2
    groups = lax.axis_size("tm")
    members = groups // SPANS
    chunks = bins // members // PART
    table = jnp.asarray(forward_rows(samples, bins))
    inverse = inverse_rows(samples, bins, members, segs * groups)
    inverse = inverse.reshape(members, 2, chunks, PART, samples)
    inverse = inverse.transpose(2, 0, 1, 3, 4).reshape(2 * bins, samples)
    flags = live.astype(jnp.bfloat16)
    next_flags = from_behind(flags, "chan", -1)
    ext_flags = jnp.concatenate([flags, next_flags], axis=0).astype(jnp.float32)
    rows = block // SPANS
    span = lax.axis_index("tm") // members
    span_flags = lax.dynamic_slice(flags.astype(jnp.float32), (span * rows,), (rows,))[::-1]
    white = whiten(traces, table, members).reshape(chunks, members, PART, 2 * segs, block)
    stack = exchange(white, span_flags, ext_flags)
    lagged = lax.dot_general(
        stack.reshape(2 * bins, block // groups * block),
        jnp.asarray(inverse),
        (((0,), (0,)), ((), ())),
        preferred_element_type=jnp.float32,
    )
    return lagged.astype(jnp.bfloat16).reshape(block // groups, block, samples)


def solution(mesh):
    in_specs = (P("tm", "chan", None), P("chan"))
    out_specs = P(("chan", "tm"), None, None)
    return jax.shard_map(body, mesh=mesh, in_specs=in_specs, out_specs=out_specs, check_vma=False)
```
